512 devices in a mesh: band: 8 (over x, core), pw: 64 (over z, y).
Axes of the slice: x: 4, y: 4, z: 16, core: 2. Of those that a mesh axis runs over, the one named last changes fastest.
Arguments:
- orbital_coefficients: float32 [8, 2, 128, 128, 128], P('band', None, 'pw'), may hold values from -6 to 6
- sphere_halfwidth: int32 [128, 128], P('pw'), may hold values from -1 to 63, as said below
- occupation: float32 [8], P('band'), may hold values from 0.5 to 2
- local_potential: float32 [256, 256, 256], P(None, 'pw'), may hold values from -6 to 6
- stencil_corner: int32 [64, 64, 128], P('pw'), may hold values from 0 to 262143, as said below
- stencil_weight: float32 [8, 64, 64, 128], P(None, 'pw'), may hold values from -3 to 3
- point_count: int32 [64, 64], P('pw'), may hold values from 0 to 128, as said below
Outputs:
- local_action: float32 [8, 2, 128, 128, 128], P('band', None, 'pw')
- fit_potential: float32 [64, 64, 128], P('pw')
The draws below stay inside these ranges and needn't reach their ends.
Inputs may be any that keep to these rules, and one draw needn't show every extreme that they name: `sphere_halfwidth`: in every draw the kept columns form one sphere centred at frequency zero that reaches the cube's faces; -1 marks an empty column. `stencil_corner`: each corner is x * 4 + y times 256 plus z, with x and z in 0 to 255 and y in 0 to 3. `point_count`: in every draw some tile has all 128 slots live from every source, and every source has some block with all 128 slots live.
All inputs are finite; a program needn't handle non-finite values.
Results may differ from the reference program's by a relative error of at most 0.0003.
Values sent between devices are 32-bit elements; how exact they have to be, the bound alone decides.
A program may use at most 64 MiB of HBM per device.

```python
import jax
import jax.numpy as jnp
from jax import lax

NG = 256
WG = 128
CAP = 128
BANDS = 8
SLAB = 4
TILES = 64
N_PW = 64


def draw_sphere_halfwidth(key, part):
    lower = (WG // 2 - 1) ** 2
    upper = (WG // 2) ** 2
    radius_sq = jax.random.randint(jax.random.fold_in(key, 11), (), lower, upper)
    frequency = jnp.arange(WG, dtype=jnp.int32) - WG // 2
    plane_sq = frequency[:, None] ** 2 + frequency[None, :] ** 2
    steps_z = jnp.arange(WG // 2, dtype=jnp.int32)
    inside = plane_sq[:, :, None] + steps_z[None, None, :] ** 2 <= radius_sq
    return (jnp.sum(inside.astype(jnp.int32), axis=2) - 1).astype(jnp.int32)


def draw_stencil_corner(key, part):
    first_key, second_key, third_key, spot_key = jax.random.split(jax.random.fold_in(key, 23), 4)
    shape_all = (TILES, TILES, CAP)
    coord_x = jax.random.randint(first_key, shape_all, 0, NG)
    coord_y = jax.random.randint(second_key, shape_all, 0, SLAB)
    coord_z = jax.random.randint(third_key, shape_all, 0, NG)
    corners = ((coord_x * SLAB + coord_y) * NG + coord_z).reshape(-1)
    spot = jax.random.randint(spot_key, (), 0, TILES * TILES * CAP)
    corners = jnp.where(jnp.arange(TILES * TILES * CAP, dtype=jnp.int32) == spot, NG * NG * SLAB - 1, corners)
    return corners.reshape(shape_all).astype(jnp.int32)


def draw_point_count(key, part):
    load_key, raw_key, full_key, own_key = jax.random.split(jax.random.fold_in(key, 37), 4)
    loads = jax.random.randint(load_key, (TILES,), 1, 5)
    raw_counts = jax.random.randint(raw_key, (TILES, TILES), 0, CAP)
    counts = jnp.minimum(CAP, raw_counts * loads[None, :] // 2)
    tile_ids = jnp.arange(TILES, dtype=jnp.int32)
    full_tile = jax.random.randint(full_key, (), 0, TILES)
    counts = jnp.where(tile_ids[None, :] == full_tile, CAP, counts)
    own_full = jax.random.randint(own_key, (TILES,), 0, TILES)
    counts = jnp.where(tile_ids[None, :] == own_full[:, None], CAP, counts)
    return counts.astype(jnp.int32)


def block_scale(key, dims, shards, smallest, top_value):
    gain, own = 1.0, jax.random.fold_in(key, 6)
    for axis_at, blocks in shards:
        draws = jnp.exp(jax.random.uniform(jax.random.fold_in(own, axis_at), (blocks,), jnp.float32, smallest / len(shards), top_value / len(shards)))
        gain = gain * jnp.repeat(draws, dims[axis_at] // blocks).reshape([-1 if axis == axis_at else 1 for axis in range(len(dims))])
    return gain


def bell_draw(key, dims, spread, limit, cuts=(), held_as=jnp.bfloat16):
    entries = spread * jax.random.normal(key, dims, jnp.float32)
    if cuts:
        entries = entries * block_scale(key, dims, cuts, -0.22, 0.18)
    return jnp.clip(entries, -limit, limit).astype(held_as)


def setup_inputs(seed: int = 0) -> dict:
    seeds = jax.random.split(jax.random.key(seed), 8)
    orbital_coefficients = bell_draw(seeds[0], (BANDS, 2, WG, WG, WG), 1.0, 6.0, ((0, 8), (2, 64)), jnp.float32)
    sphere_halfwidth = draw_sphere_halfwidth(jax.random.fold_in(seeds[7], 71), 0)
    occupation = jnp.clip(0.5 + 1.5 * jax.random.uniform(seeds[2], (BANDS,), jnp.float32) ** block_scale(seeds[2], (BANDS,), ((0, 8),), -0.2, 0.2), 0.5, 2.0)
    local_potential = bell_draw(seeds[3], (NG, NG, NG), 1.0, 6.0, ((1, 64),), jnp.float32)
    stencil_corner = draw_stencil_corner(jax.random.fold_in(seeds[7], 71), 0)
    stencil_weight = bell_draw(seeds[5], (8, TILES, TILES, CAP), 0.5, 3.0, ((1, 64),), jnp.float32)
    point_count = draw_point_count(jax.random.fold_in(seeds[7], 71), 0)
    return dict(orbital_coefficients=orbital_coefficients, sphere_halfwidth=sphere_halfwidth, occupation=occupation, local_potential=local_potential, stencil_corner=stencil_corner, stencil_weight=stencil_weight, point_count=point_count)


hartree_scale = 200.0


def reference(orbital_coefficients, sphere_halfwidth, occupation, local_potential, stencil_corner, stencil_weight, point_count):
    frequency = jnp.arange(WG, dtype=jnp.int32) - WG // 2
    sphere_mask = (jnp.abs(frequency)[None, None, :] <= sphere_halfwidth[:, :, None]).astype(jnp.float32)
    cube_index = jnp.remainder(frequency, NG).astype(jnp.int32)
    scale_in = float(WG) ** -1.5
    scale_out = float(WG) ** 1.5 / float(NG) ** 3
    density = jnp.zeros((NG, NG, NG), jnp.float32)
    results = []
    for band_index in range(BANDS):
        coefficient = lax.complex(orbital_coefficients[band_index, 0] * sphere_mask, orbital_coefficients[band_index, 1] * sphere_mask)
        full_grid = jnp.zeros((NG, NG, NG), coefficient.dtype)
        full_grid = full_grid.at[cube_index[:, None, None], cube_index[None, :, None], cube_index[None, None, :]].set(coefficient)
        orbital = jnp.fft.ifftn(full_grid) * (float(NG) ** 3 * scale_in)
        density = density + occupation[band_index] * (orbital.real ** 2 + orbital.imag ** 2)
        spectrum = jnp.fft.fftn(local_potential * orbital)
        picked = spectrum[cube_index[:, None, None], cube_index[None, :, None], cube_index[None, None, :]] * scale_out
        results.append(jnp.stack([picked.real * sphere_mask, picked.imag * sphere_mask]))
    local_action = jnp.stack(results)
    grid_freq = jnp.arange(NG, dtype=jnp.int32)
    signed = jnp.where(grid_freq < NG // 2, grid_freq, grid_freq - NG)
    square = signed[:, None, None] ** 2 + signed[None, :, None] ** 2 + signed[None, None, :] ** 2
    kernel = jnp.where(square > 0, hartree_scale / jnp.maximum(square, 1).astype(jnp.float32), 0.0)
    hartree = jnp.fft.ifftn(jnp.fft.fftn(density) * kernel).real
    slab_depth = NG // N_PW
    coord_x = stencil_corner // (slab_depth * NG)
    coord_y = (stencil_corner // NG) % slab_depth
    coord_z = stencil_corner % NG
    tile_index = jnp.arange(N_PW, dtype=jnp.int32)[None, :, None]
    summed = jnp.zeros(stencil_corner.shape, jnp.float32)
    for corner in range(8):
        step_x = corner // 4
        step_y = (corner // 2) % 2
        step_z = corner % 2
        cell_x = (coord_x + step_x) % NG
        cell_y = (tile_index * slab_depth + coord_y + step_y) % NG
        cell_z = (coord_z + step_z) % NG
        summed = summed + stencil_weight[corner] * hartree[cell_x, cell_y, cell_z]
    live_slot = jnp.arange(CAP, dtype=jnp.int32)[None, None, :] < point_count[:, :, None]
    fit_potential = jnp.where(live_slot, summed, 0.0)
    return local_action, fit_potential
```

```python
import math

import jax
import jax.numpy as jnp
import numpy as np
from jax import lax
from jax.sharding import PartitionSpec as P

HARTREE_SCALE = 200.0
HIGH = lax.Precision.HIGH


def wave_table(positions, modes, grid):
    angle = (np.outer(positions, modes) % grid) * (2.0 * math.pi / grid)
    cosine, sine = np.cos(angle), np.sin(angle)
    return np.stack([np.stack([cosine, -sine], 1), np.stack([sine, cosine], 1)], 0)


def real_basis(grid):
    half = grid // 2
    position = np.arange(grid)
    angle = lambda n: (np.outer(n, position) % grid) * (2.0 * math.pi / grid)
    rows = np.concatenate([np.cos(angle(np.arange(half + 1))), np.sin(angle(np.arange(1, half)))])
    return rows / np.sqrt(np.sum(rows * rows, axis=1, keepdims=True))


def dot(spec, *operands):
    return jnp.einsum(spec, *operands, precision=HIGH, preferred_element_type=jnp.float32)


def body(coefficients, halfwidth, occupation, potential, corner, weight, count):
    wg = coefficients.shape[3]
    ng = potential.shape[0]
    slab = potential.shape[1]
    slots = corner.shape[2]
    bands = lax.axis_size("band")
    tiles = lax.axis_size("pw")
    b = lax.axis_index("band")
    p = lax.axis_index("pw")
    f32 = lambda a: jnp.asarray(a, jnp.float32)
    modes = np.arange(wg) - wg // 2
    wave = wave_table(np.arange(ng), modes, ng)
    scale_in = float(wg) ** -1.5
    scale_out = float(wg) ** 1.5 / float(ng) ** 3
    cube = f32(wave)
    wave_y = f32(wave.reshape(2, tiles, slab, 2, wg))
    mask = (jnp.abs(f32(modes))[None, None, :] <= halfwidth[:, :, None]).astype(jnp.float32)

    share = slots // bands
    packed = jnp.concatenate([weight[:, 0], corner[0].astype(jnp.float32)[None]], 0)
    packed = lax.dynamic_slice_in_dim(packed, b * share, share, 2)
    packed = packed.transpose(1, 0, 2).reshape(tiles, 9 * share)
    packed = lax.all_to_all(packed, "pw", 0, 0, tiled=True)

    masked = coefficients[0] * (mask * scale_in)[None]
    section = dot("edjcm,cimz->deijz", wave_y, masked)
    section = lax.all_to_all(section, "pw", 0, 0, tiled=True)
    cube_x = cube.reshape(2, ng, 2, tiles, wg // tiles)
    section = dot("excpi,pcijz->exjz", cube_x, section)
    orbital = dot("fzcm,cxjm->fxjz", cube, section)
    density = occupation[0] * (orbital[0] ** 2 + orbital[1] ** 2)

    basis_np = real_basis(ng)
    basis = f32(basis_np)
    first = jnp.arange(ng) == 0
    mean = jnp.mean(density, axis=(0, 2))
    spectrum = dot("xjz,lz->xjl", density - mean[None, :, None], basis)
    spectrum = dot("kx,xjl->kjl", basis, spectrum)
    spectrum = spectrum + jnp.where(first[:, None, None] & first[None, None, :], float(ng) * mean[None, :, None], 0.0)
    spectrum = lax.psum_scatter(spectrum, "band", scatter_dimension=0, tiled=True)
    per = ng // bands
    halves = tiles // per
    lanes = ng // halves
    spectrum = spectrum.reshape(per, slab, halves, lanes).transpose(0, 2, 1, 3).reshape(tiles, slab, lanes)
    spectrum = lax.all_to_all(spectrum, "pw", 0, 0, tiled=True).reshape(ng, lanes)
    mean = jnp.mean(spectrum, axis=0)
    spectrum = dot("ky,yl->kl", basis, spectrum - mean[None])
    spectrum = spectrum + jnp.where(first[:, None], math.sqrt(ng) * mean[None], 0.0)
    number = jnp.arange(ng, dtype=jnp.int32)
    number = jnp.where(number <= ng // 2, number, number - ng // 2)
    take = lambda start, size: lax.dynamic_slice_in_dim(number, start, size)
    square = (
        number[:, None] ** 2
        + take((p % halves) * lanes, lanes)[None, :] ** 2
        + take(b * per + p // halves, 1)[:, None] ** 2
    )
    kernel = jnp.where(square > 0, HARTREE_SCALE / jnp.maximum(square, 1).astype(jnp.float32), 0.0)
    planes = (np.arange(tiles)[:, None] * slab + np.arange(slab + 1)[None, :]) % ng
    back = f32(basis_np.T[planes])
    spectrum = dot("tjk,kl->tjl", back, spectrum * kernel)
    spectrum = lax.all_to_all(spectrum, "pw", 0, 0, tiled=True)
    spectrum = lax.all_gather(spectrum, "band", axis=0, tiled=True)
    spectrum = spectrum.reshape(ng, halves, slab + 1, lanes)
    basis_z = basis.reshape(halves, lanes, ng)
    hartree = dot("khjl,hlz->kjz", spectrum, basis_z)
    hartree = dot("kx,kjz->zjx", basis, hartree)

    product = orbital * potential[None]
    product = dot("fzcm,fxjz->cxjm", cube, product)
    product = dot("excpi,exjz->pcijz", cube_x, product)
    product = lax.all_to_all(product, "pw", 0, 0, tiled=True)
    action = dot("edjcm,deijz->cimz", wave_y, product)
    action = action * (mask * scale_out)[None]

    packed = packed.reshape(tiles, 9, share).transpose(1, 0, 2).reshape(9, tiles * share)
    place = packed[8].astype(jnp.int32)
    px, py, pz = place // (slab * ng), place // ng % slab, place % ng
    index_x = jnp.arange(ng, dtype=jnp.int32)
    index_y = jnp.arange(slab + 1, dtype=jnp.int32)
    total = 0.0
    for dz in range(2):
        column = 0.0
        for dx in range(2):
            at_x = index_x[:, None] == ((px + dx) % ng)[None, :]
            for dy in range(2):
                at_y = index_y[:, None] == (py + dy)[None, :]
                w = packed[4 * dx + 2 * dy + dz]
                column = column + jnp.where(at_y[:, None] & at_x[None], w[None, None], 0.0)
        lines = dot("zjx,jxs->zs", hartree, column)
        at_z = index_x[:, None] == ((pz + dz) % ng)[None, :]
        total = total + jnp.sum(jnp.where(at_z, lines, 0.0), axis=0)
    total = lax.all_to_all(total.reshape(tiles, share), "pw", 0, 0, tiled=True)
    total = lax.all_gather(total, "band", axis=1, tiled=True)
    live = jnp.arange(slots, dtype=jnp.int32)[None, :] < count[0][:, None]
    return action[None], jnp.where(live, total, 0.0)[None]


def solution(mesh):
    placed = (
        P("band", None, "pw", None, None),
        P("pw", None),
        P("band"),
        P(None, "pw", None),
        P("pw", None, None),
        P(None, "pw", None, None),
        P("pw", None),
    )
    return jax.shard_map(
        body,
        mesh=mesh,
        in_specs=placed,
        out_specs=(P("band", None, "pw", None, None), P("pw", None, None)),
        check_vma=False,
    )
```

```python
import math

import jax
import jax.numpy as jnp
import ml_dtypes
import numpy as np
from jax import lax
from jax.experimental import pallas as pl
from jax.experimental.pallas import tpu as pltpu
from jax.sharding import PartitionSpec as P

HARTREE_SCALE = 200.0
MESH = pl.DeviceIdType.MESH
F32 = jnp.float32
BF16 = jnp.bfloat16

NG = 256
WG = 128
BANDS = 8
TILES = 64
SLAB = 4
CAP = 128
PER = NG // BANDS
SRC = TILES // BANDS
SCALE_IN = float(WG) ** -1.5
SCALE_OUT = float(WG) ** 1.5 / float(NG) ** 3


def halves_of(table):
    high = np.asarray(table, np.float64).astype(ml_dtypes.bfloat16)
    low = (table - high.astype(np.float64)).astype(ml_dtypes.bfloat16)
    return np.stack([high, low])


def tables():
    position = np.arange(NG)
    modes = np.arange(WG) - WG // 2
    angle = (np.outer(position, modes) % NG) * (2.0 * math.pi / NG)
    cosine, sine = np.cos(angle), np.sin(angle)
    wave = np.stack([np.stack([cosine, -sine], 1), np.stack([sine, cosine], 1)], 0)
    wave_y = wave.reshape(2, TILES, SLAB, 2, WG).transpose(1, 0, 2, 3, 4).reshape(2 * NG, 2 * WG)
    wave_x = wave.reshape(2, NG, 2, TILES, 2).transpose(0, 1, 2, 4, 3).reshape(2 * NG, 2 * WG)
    wave_z = wave.transpose(2, 3, 0, 1).reshape(2 * WG, 2 * NG)
    angle = lambda n: (np.outer(n, position) % NG) * (2.0 * math.pi / NG)
    rows = np.concatenate([np.cos(angle(np.arange(NG // 2 + 1))), np.sin(angle(np.arange(1, NG // 2)))])
    basis = rows / np.sqrt(np.sum(rows * rows, axis=1, keepdims=True))
    basis_y = basis.reshape(NG, TILES, SLAB).transpose(0, 2, 1).reshape(NG, NG)
    planes = (np.arange(TILES)[:, None] * SLAB + np.arange(8)[None, :]) % NG
    back_y = basis.T[planes] * (np.arange(8) <= SLAB)[None, :, None]
    named = dict(
        wave_y=wave_y,
        wave_x=wave_x,
        wave_z=wave_z,
        basis_t=basis.T,
        basis=basis,
        basis_y=basis_y,
        back_y=back_y.reshape(8 * TILES, NG),
        wave_zt=wave_z.T,
        wave_xt=wave_x.T,
        wave_yt=wave_y.T,
    )
    return {name: halves_of(table) for name, table in named.items()}


LATE = ("wave_x", "wave_z", "basis_t", "basis", "wave_zt", "wave_xt", "basis_y", "back_y", "wave_yt")


def split(value):
    high = value.astype(BF16)
    return high, (value - high.astype(F32)).astype(BF16)


def dot3(left, right, last=False):
    dims = (((1,), (1 if last else 0,)), ((), ()))
    one = lambda a, b: lax.dot_general(a, b, dims, preferred_element_type=F32)
    return one(left[0], right[0]) + (one(left[0], right[1]) + one(left[1], right[0]))


def pair(ref):
    return ref[0], ref[1]


def iota(shape, dim):
    return lax.broadcasted_iota(jnp.int32, shape, dim)


def as_column(row):
    size = row.shape[1]
    on = iota((size, size), 0) == iota((size, size), 1)
    return jnp.sum(jnp.where(on, jnp.broadcast_to(row, (size, size)), 0.0), axis=1, keepdims=True)


def drain(ref, sem):
    pltpu.make_async_copy(ref, ref, sem).wait()


def kernel(
    coef, half, occupation, count, wave_y,
    potential, corner, weight, wave_x_h, wave_z_h, basis_t_h, basis_h, wave_zt_h, wave_xt_h,
    basis_y_h, back_y_h, wave_yt_h,
    action, fit,
    wave_x, wave_z, basis_t, basis, wave_zt, wave_xt, basis_y, back_y, wave_yt,
    pot, corn, weig,
    s1, r1, s2, r2, bx, lz, psi, ez, sr, rs1, rs2, ss, ys, sb, g, green, pk, pr, wst, ht, stage, o, f,
    load_sem, a1, a2, pt_s, pt_r, t1_s, t1_r, t2_s, t2_r, sf, bk, g1_s, g1_r, g2_s, g2_r, fin,
):
    b = lax.axis_index("band")
    p = lax.axis_index("pw")
    x, c = b // 2, b % 2
    partner = b + 1 - 2 * c
    heavy = p // SRC == b

    loads = []
    for j in range(SLAB):
        loads.append((potential.at[:, j, :], pot.at[j]))
    for source, target in (
        (corner, corn), (weight, weig), (wave_x_h, wave_x), (wave_z_h, wave_z), (basis_t_h, basis_t), (basis_h, basis),
        (wave_zt_h, wave_zt), (wave_xt_h, wave_xt), (basis_y_h, basis_y), (back_y_h, back_y), (wave_yt_h, wave_yt),
    ):
        loads.append((source, target))
    loads = [pltpu.make_async_copy(a, z, load_sem.at[n]) for n, (a, z) in enumerate(loads)]
    for load in loads:
        load.start()

    barrier = pltpu.get_barrier_semaphore()

    def greet_pw(k, _):
        pl.semaphore_signal(barrier, inc=1, device_id={"pw": lax.rem(p + k, TILES)}, device_id_type=MESH)
        return 0

    lax.fori_loop(1, TILES, greet_pw, 0)

    def greet_band(k, _):
        pl.semaphore_signal(barrier, inc=1, device_id={"band": lax.rem(b + k, BANDS)}, device_id_type=MESH)
        return 0

    lax.fori_loop(1, BANDS, greet_band, 0)

    def greet_fit(q, _):
        @pl.when(jnp.logical_not(jnp.logical_and(heavy, q == p)))
        def _():
            pl.semaphore_signal(barrier, inc=1, device_id={"band": p // SRC, "pw": q}, device_id_type=MESH)
        return 0

    lax.fori_loop(0, TILES, greet_fit, 0)

    lane = iota((WG, WG), 1)
    masks = []
    for i in range(2):
        reach = as_column(half[i : i + 1, :].astype(F32))
        masks.append(jnp.where(jnp.abs(lane - WG // 2).astype(F32) <= reach, 1.0, 0.0))
    rows = [
        jnp.concatenate([coef[0, k, i] * (masks[i] * SCALE_IN) for i in range(2)], axis=1) for k in range(2)
    ]
    section = dot3(pair(wave_y), split(jnp.concatenate(rows, axis=0)))
    for i in range(2):
        s1[:, i] = section[:, i * WG : (i + 1) * WG].reshape(TILES, 8, WG)

    @pl.when(heavy)
    def _():
        pl.semaphore_wait(barrier, TILES - 1 + BANDS - 1 + TILES - 1)

    @pl.when(jnp.logical_not(heavy))
    def _():
        pl.semaphore_wait(barrier, TILES - 1 + BANDS - 1 + TILES)

    def exchange(source, target, sems):
        def send(k, _):
            q = lax.rem(p + k, TILES)
            pltpu.make_async_remote_copy(
                source(q), target(p), sems.at[0], sems.at[1], device_id={"pw": q}, device_id_type=MESH
            ).start()
            return 0

        lax.fori_loop(1, TILES, send, 0)

    exchange(lambda q: s1.at[q], lambda q: r1.at[q], a1)
    r1[p] = s1[p]

    loads[SLAB].wait()
    loads[SLAB + 1].wait()

    @pl.when(heavy)
    def _():
        flat = pk.reshape(TILES * 16, CAP)
        for k in range(8):
            flat[pl.ds(k, TILES, stride=16), :] = weig[k, 0]
        flat[pl.ds(8, TILES, stride=16), :] = corn[0].astype(F32)

    mode = lambda k: jnp.where(k <= NG // 2, k, k - NG // 2)
    n_y = mode(iota((NG, CAP), 0))
    n_z = mode((p // PER) * CAP + iota((NG, CAP), 1))
    n_x = mode(b * PER + lax.rem(p, PER))
    square = n_y * n_y + n_z * n_z + n_x * n_x
    green[...] = jnp.where(square > 0, HARTREE_SCALE / jnp.maximum(square, 1).astype(F32), 0.0)

    for load in loads[:SLAB] + loads[SLAB + 2 :]:
        load.wait()

    drain(r1.at[pl.ds(0, TILES - 1)], a1.at[1])

    @pl.when(heavy)
    def _():
        def send(k, _):
            q = lax.rem(p + k, TILES)
            pltpu.make_async_remote_copy(
                pk.at[q, pl.ds(0, 9)], pr.at[p % SRC, pl.ds(0, 9)], pt_s, pt_r.at[p % SRC],
                device_id={"pw": q}, device_id_type=MESH,
            ).start()
            return 0

        lax.fori_loop(1, TILES, send, 0)
        pr[p % SRC, 0:9] = pk[p, 0:9]

    flat = r1.reshape(TILES * 16, WG)
    for k in range(2):
        for i in range(2):
            for j in range(SLAB):
                high, low = split(flat[pl.ds(i * 8 + k * SLAB + j, TILES, stride=16), :])
                at = (pl.ds(k * WG + i * TILES, TILES), pl.ds(j * WG, WG))
                bx[(0,) + at] = high
                bx[(1,) + at] = low
    turned = dot3(pair(wave_x), pair(bx))
    for j in range(SLAB):
        for k in range(2):
            high, low = split(turned[k * NG : (k + 1) * NG, j * WG : (j + 1) * WG])
            lz[j, 0, :, k * WG : (k + 1) * WG] = high
            lz[j, 1, :, k * WG : (k + 1) * WG] = low

    corner_on = jnp.logical_and(iota((NG, NG), 0) == 0, iota((NG, NG), 1) == 0)

    def density_step(j, _):
        orbital = dot3((lz[j, 0], lz[j, 1]), pair(wave_z))
        psi[j] = orbital
        real, imag = orbital[:, :NG], orbital[:, NG:]
        density = occupation[0] * (real * real + imag * imag)
        mean = jnp.sum(jnp.sum(density, axis=0, keepdims=True), axis=1, keepdims=True) * (1.0 / (NG * NG))
        modes = dot3(split(density - mean), pair(basis_t))
        modes = dot3(pair(basis), split(modes))
        modes = modes + jnp.where(corner_on, NG * mean, 0.0)
        sr[j] = modes.reshape(BANDS // 2, 2, PER, NG)
        pltpu.make_async_remote_copy(
            sr.at[j, :, 1 - c], rs1.at[j], t1_s.at[j], t1_r.at[j], device_id={"band": partner}, device_id_type=MESH
        ).start()
        return 0

    lax.fori_loop(0, SLAB, density_step, 0)

    def across(j, _):
        drain(rs1.at[j], t1_r.at[j])
        for k in range(BANDS // 2):
            rs1[j, k] = rs1[j, k] + sr[j, k, c]

        def send(k, _):
            to = lax.rem(x + k, BANDS // 2)
            pltpu.make_async_remote_copy(
                rs1.at[j, to], rs2.at[j, x], t2_s.at[j], t2_r.at[j],
                device_id={"band": 2 * to + c}, device_id_type=MESH,
            ).start()
            return 0

        lax.fori_loop(1, BANDS // 2, send, 0)
        rs2[j, x] = rs1[j, x]
        return 0

    lax.fori_loop(0, SLAB, across, 0)

    def product_step(j, _):
        value = pot[j]
        field = psi[j] * jnp.concatenate([value, value], axis=1)
        ez[j] = dot3(split(field), pair(wave_zt))
        return 0

    lax.fori_loop(0, SLAB, product_step, 0)

    flat_s = ss.reshape(TILES * 8, CAP)

    def gather_bands(j, _):
        drain(rs2.at[j, pl.ds(0, BANDS // 2 - 1)], t2_r.at[j])
        total = (rs2[j, 0] + rs2[j, 1]) + (rs2[j, 2] + rs2[j, 3])
        for h in range(2):
            flat_s[pl.ds(h * PER * 8 + j, PER, stride=8), :] = total[:, h * CAP : (h + 1) * CAP]
        return 0

    for j in range(SLAB):
        gather_bands(j, 0)

    four = pl.ds(0, SLAB)
    exchange(lambda q: ss.at[q, four], lambda q: ys.at[q, four], sf)
    ys[p, 0:SLAB] = ss[p, 0:SLAB]

    cols = [jnp.concatenate([ez[j, :, k * WG : (k + 1) * WG] for j in range(SLAB)], axis=1) for k in range(2)]
    cube = dot3(pair(wave_xt), split(jnp.concatenate(cols, axis=0)))
    flat = s2.reshape(TILES * 16, WG)
    for k in range(2):
        for i in range(2):
            for j in range(SLAB):
                at = k * WG + i * TILES
                flat[pl.ds(i * 8 + k * SLAB + j, TILES, stride=16), :] = cube[at : at + TILES, j * WG : (j + 1) * WG]

    drain(ys.at[pl.ds(0, TILES - 1), four], sf.at[1])
    flat_y = ys.reshape(TILES * 8, CAP)
    lines = jnp.concatenate([flat_y[pl.ds(j, TILES, stride=8), :] for j in range(SLAB)], axis=0)
    mean = jnp.sum(lines, axis=0, keepdims=True) * (1.0 / NG)
    modes = dot3(pair(basis_y), split(lines - mean))
    modes = modes + jnp.where(iota((NG, CAP), 0) == 0, math.sqrt(NG) * mean, 0.0)
    sb[...] = dot3(pair(back_y), split(modes * green[...])).reshape(TILES, 8, CAP)
    five = pl.ds(0, SLAB + 1)
    exchange(lambda q: sb.at[q, five], lambda q: g.at[b, q, five], bk)
    g[b, p] = sb[p]
    exchange(lambda q: s2.at[q], lambda q: r2.at[q], a2)
    r2[p] = s2[p]

    def point_step(i, _):
        source = SRC * b + i

        @pl.when(source != p)
        def _():
            drain(pr.at[i, pl.ds(0, 9)], pt_r.at[i])

        data = pr[i, 0:9]
        place = data[8:9].astype(jnp.int32)
        at_x = place // (SLAB * NG)
        at_y = lax.rem(place // NG, SLAB)
        across_x = iota((NG, CAP), 0)
        on = [across_x == at_x, across_x == lax.rem(at_x + 1, NG)]
        for y in range(SLAB + 1):
            for dz in range(2):
                value = []
                for dx in range(2):
                    first = jnp.where(at_y == y, data[4 * dx + dz : 4 * dx + dz + 1], 0.0)
                    value.append(jnp.where(at_y == y - 1, data[4 * dx + 2 + dz : 4 * dx + 3 + dz], first))
                value = jnp.where(on[0], value[0], jnp.where(on[1], value[1], 0.0))
                high, low = split(value)
                wst[i, 0, y * NG : (y + 1) * NG, dz * CAP : (dz + 1) * CAP] = high
                wst[i, 1, y * NG : (y + 1) * NG, dz * CAP : (dz + 1) * CAP] = low
        return 0

    lax.fori_loop(0, SRC, point_step, 0)

    drain(g.at[b, pl.ds(0, TILES - 1), five], bk.at[1])

    def pass_on(k):
        block = lax.rem(x + BANDS // 2 - k, BANDS // 2) * 2 + c
        pltpu.make_async_remote_copy(
            g.at[block, :, five], g.at[block, :, five], g2_s.at[k], g2_r.at[k],
            device_id={"band": partner}, device_id_type=MESH,
        ).start()

    def send_x(k, _):
        to = lax.rem(x + k, BANDS // 2)
        pltpu.make_async_remote_copy(
            g.at[b, :, five], g.at[b, :, five], g1_s.at[k], g1_r.at[k],
            device_id={"band": 2 * to + c}, device_id_type=MESH,
        ).start()
        return 0

    lax.fori_loop(1, BANDS // 2, send_x, 0)
    pass_on(0)

    def forward(k, _):
        block = lax.rem(x + BANDS // 2 - k, BANDS // 2) * 2 + c
        drain(g.at[block, :, five], g1_r.at[k])
        pass_on(k)
        return 0

    lax.fori_loop(1, BANDS // 2, forward, 0)

    def arrived(k, _):
        block = lax.rem(x + BANDS // 2 - k, BANDS // 2) * 2 + 1 - c
        drain(g.at[block, :, five], g2_r.at[k])
        return 0

    lax.fori_loop(0, BANDS // 2, arrived, 0)

    flat_g = g.reshape(BANDS * TILES * 8, CAP)
    for y in range(SLAB + 1):
        for h in range(2):
            for n in range(BANDS):
                high, low = split(flat_g[pl.ds(n * TILES * 8 + h * PER * 8 + y, PER, stride=8), :])
                stage[0, n * PER : (n + 1) * PER, h * CAP : (h + 1) * CAP] = high
                stage[1, n * PER : (n + 1) * PER, h * CAP : (h + 1) * CAP] = low
        plane = dot3(pair(basis_t), pair(stage))
        plane = dot3(pair(basis_t), split(plane), last=True)
        high, low = split(plane)
        ht[0, :, y * NG : (y + 1) * NG] = high
        ht[1, :, y * NG : (y + 1) * NG] = low

    def fit_step(i, _):
        lines = dot3(pair(ht), (wst[i, 0], wst[i, 1]))
        at_z = lax.rem(pr[i, 8:9].astype(jnp.int32), NG)
        at_z = jnp.concatenate([at_z, lax.rem(at_z + 1, NG)], axis=1)
        lines = jnp.sum(jnp.where(iota((NG, 2 * CAP), 0) == at_z, lines, 0.0), axis=0, keepdims=True)
        o[i] = lines[:, :CAP] + lines[:, CAP:]
        return 0

    lax.fori_loop(0, SRC, fit_step, 0)

    def fit_send(n, _):
        to, i = n // SRC, lax.rem(n, SRC)

        @pl.when(jnp.logical_not(jnp.logical_and(to == b, SRC * b + i == p)))
        def _():
            pltpu.make_async_remote_copy(
                o.at[i], f.at[p], fin.at[0], fin.at[1],
                device_id={"band": to, "pw": SRC * b + i}, device_id_type=MESH,
            ).start()
        return 0

    lax.fori_loop(0, BANDS * SRC, fit_send, 0)

    @pl.when(heavy)
    def _():
        f[p] = o[p % SRC]

    drain(r2.at[pl.ds(0, TILES - 1)], a2.at[1])
    cube = jnp.concatenate([r2[:, i].reshape(TILES * 8, WG) for i in range(2)], axis=1)
    cube = dot3(pair(wave_yt), split(cube))
    for k in range(2):
        for i in range(2):
            action[0, k, i] = cube[k * WG : (k + 1) * WG, i * WG : (i + 1) * WG] * (masks[i] * SCALE_OUT)

    @pl.when(heavy)
    def _():
        drain(f.at[pl.ds(0, TILES - 1)], fin.at[1])
        drain(f.at[pl.ds(0, TILES - 1)], fin.at[0])

    @pl.when(jnp.logical_not(heavy))
    def _():
        drain(f, fin.at[1])
        drain(f, fin.at[0])

    live = iota((TILES, CAP), 1).astype(F32) < as_column(count[...].astype(F32))
    fit[0] = jnp.where(live, f[...].reshape(TILES, CAP), 0.0)

    drain(s1.at[pl.ds(0, TILES - 1)], a1.at[0])
    drain(s2.at[pl.ds(0, TILES - 1)], a2.at[0])
    drain(ss.at[pl.ds(0, TILES - 1), four], sf.at[0])
    drain(sb.at[pl.ds(0, TILES - 1), five], bk.at[0])

    @pl.when(heavy)
    def _():
        drain(pk.at[pl.ds(0, TILES - 1), pl.ds(0, 9)], pt_s)

    def sent(j, _):
        drain(rs1.at[j], t1_s.at[j])
        drain(rs1.at[j, pl.ds(0, BANDS // 2 - 1)], t2_s.at[j])
        return 0

    lax.fori_loop(0, SLAB, sent, 0)

    def passed(k, _):
        drain(g.at[b, :, five], g2_s.at[k])

        @pl.when(k > 0)
        def _():
            drain(g.at[b, :, five], g1_s.at[k])
        return 0

    lax.fori_loop(0, BANDS // 2, passed, 0)


def body(coefficients, halfwidth, occupation, potential, corner, weight, count):
    held = {name: jnp.asarray(table) for name, table in tables().items()}
    late = [held[name] for name in LATE]
    vmem = pl.BlockSpec(memory_space=pltpu.VMEM)
    anywhere = pl.BlockSpec(memory_space=pl.ANY)
    dma = pltpu.SemaphoreType.DMA
    block = lambda *shape: pltpu.VMEM(shape, F32)
    short = lambda *shape: pltpu.VMEM(shape, BF16)
    scratch = [short(*table.shape) for table in late]
    scratch += [
        block(SLAB, NG, NG),
        pltpu.VMEM((1, TILES, CAP), jnp.int32),
        block(8, 1, TILES, CAP),
        block(TILES, 2, 8, WG),
        block(TILES, 2, 8, WG),
        block(TILES, 2, 8, WG),
        block(TILES, 2, 8, WG),
        short(2, 2 * WG, SLAB * WG),
        short(SLAB, 2, NG, 2 * WG),
        block(SLAB, NG, 2 * NG),
        block(SLAB, NG, 2 * WG),
        block(SLAB, BANDS // 2, 2, PER, NG),
        block(SLAB, BANDS // 2, PER, NG),
        block(SLAB, BANDS // 2, PER, NG),
        block(TILES, 8, CAP),
        block(TILES, 8, CAP),
        block(TILES, 8, CAP),
        block(BANDS, TILES, 8, CAP),
        block(NG, CAP),
        block(TILES, 16, CAP),
        block(SRC, 16, CAP),
        short(SRC, 2, (SLAB + 1) * NG, 2 * CAP),
        short(2, NG, (SLAB + 1) * NG),
        short(2, NG, NG),
        block(SRC, 1, CAP),
        block(TILES, 1, CAP),
    ]
    scratch += [
        dma((SLAB + 2 + len(late),)),
        dma((2,)), dma((2,)),
        dma(()), dma((SRC,)),
        dma((SLAB,)), dma((SLAB,)), dma((SLAB,)), dma((SLAB,)),
        dma((2,)), dma((2,)),
        dma((BANDS // 2,)), dma((BANDS // 2,)), dma((BANDS // 2,)), dma((BANDS // 2,)),
        dma((2,)),
    ]
    return pl.pallas_call(
        kernel,
        out_shape=(
            jax.ShapeDtypeStruct(coefficients.shape, F32),
            jax.ShapeDtypeStruct(corner.shape, F32),
        ),
        in_specs=[vmem, vmem, pl.BlockSpec(memory_space=pltpu.SMEM), vmem, vmem] + [anywhere] * (3 + len(late)),
        out_specs=(vmem, vmem),
        scratch_shapes=scratch,
        compiler_params=pltpu.CompilerParams(
            collective_id=0, has_side_effects=True, vmem_limit_bytes=52 * 1024 * 1024
        ),
    )(coefficients, halfwidth, occupation, count, held["wave_y"], potential, corner, weight, *late)


def solution(mesh):
    placed = (
        P("band", None, "pw", None, None),
        P("pw", None),
        P("band"),
        P(None, "pw", None),
        P("pw", None, None),
        P(None, "pw", None, None),
        P("pw", None),
    )
    return jax.shard_map(
        body,
        mesh=mesh,
        in_specs=placed,
        out_specs=(P("band", None, "pw", None, None), P("pw", None, None)),
        check_vma=False,
    )
```

```python
import math

import jax
import jax.numpy as jnp
import ml_dtypes
import numpy as np
from jax import lax
from jax.experimental import pallas as pl
from jax.experimental.pallas import tpu as pltpu
from jax.sharding import PartitionSpec as P

HARTREE_SCALE = 200.0
MESH = pl.DeviceIdType.MESH
F32 = jnp.float32
BF16 = jnp.bfloat16

NG = 256
WG = 128
BANDS = 8
TILES = 64
SLAB = 4
CAP = 128
PER = NG // BANDS
SRC = TILES // BANDS
GROUPS = (pl.ds(0, 3), pl.ds(3, 2))
SCALE_IN = float(WG) ** -1.5
SCALE_OUT = float(WG) ** 1.5 / float(NG) ** 3


def halves_of(table):
    high = np.asarray(table, np.float64).astype(ml_dtypes.bfloat16)
    low = (table - high.astype(np.float64)).astype(ml_dtypes.bfloat16)
    return np.stack([high, low])


def tables():
    position = np.arange(NG)
    modes = np.arange(WG) - WG // 2
    angle = (np.outer(position, modes) % NG) * (2.0 * math.pi / NG)
    cosine, sine = np.cos(angle), np.sin(angle)
    wave = np.stack([np.stack([cosine, -sine], 1), np.stack([sine, cosine], 1)], 0)
    wave_y = wave.reshape(2, TILES, SLAB, 2, WG).transpose(1, 2, 0, 3, 4).reshape(2 * NG, 2 * WG)
    wave_x = wave.reshape(2, NG, 2, TILES, 2).transpose(0, 1, 2, 4, 3).reshape(2 * NG, 2 * WG)
    wave_z = wave.transpose(2, 3, 0, 1).reshape(2 * WG, 2 * NG)
    angle = lambda n: (np.outer(n, position) % NG) * (2.0 * math.pi / NG)
    rows = np.concatenate([np.cos(angle(np.arange(NG // 2 + 1))), np.sin(angle(np.arange(1, NG // 2)))])
    basis = rows / np.sqrt(np.sum(rows * rows, axis=1, keepdims=True))
    basis_y = basis.reshape(NG, TILES, SLAB).transpose(0, 2, 1).reshape(NG, NG)
    planes = (np.arange(TILES)[None, :] * SLAB + np.arange(SLAB + 1)[:, None]) % NG
    named = dict(
        wave_y=wave_y,
        wave_x=wave_x,
        wave_z=wave_z,
        basis_t=basis.T,
        basis=basis,
        basis_y=basis_y,
        back_y=basis.T[planes.reshape(-1)],
        wave_zt=wave_z.T,
        wave_xt=wave_x.T,
        wave_yt=wave_y.T,
    )
    return {name: halves_of(table) for name, table in named.items()}


LATE = ("wave_y", "wave_x", "wave_z", "basis_t", "basis", "wave_zt", "wave_xt", "basis_y", "back_y", "wave_yt")


def split(value):
    high = value.astype(BF16)
    return high, (value - high.astype(F32)).astype(BF16)


def dot(left, right):
    return jnp.dot(left, right, preferred_element_type=F32)


def dot3(left, right):
    return dot(left[0], right[0]) + (dot(left[0], right[1]) + dot(left[1], right[0]))


def pair(ref):
    return ref[0], ref[1]


def iota(shape, dim):
    return lax.broadcasted_iota(jnp.int32, shape, dim)


def as_column(row):
    size = row.shape[1]
    on = iota((size, size), 0) == iota((size, size), 1)
    return jnp.sum(jnp.where(on, jnp.broadcast_to(row, (size, size)), 0.0), axis=1, keepdims=True)


def drain(ref, sem):
    pltpu.make_async_copy(ref, ref, sem).wait()


def kernel(
    half, occupation, count,
    coef_h, wave_y_h, potential, corner, weight, wave_x_h, wave_z_h, basis_t_h, basis_h, wave_zt_h, wave_xt_h,
    basis_y_h, back_y_h, wave_yt_h,
    action, fit,
    wave_y, wave_x, wave_z, basis_t, basis, wave_zt, wave_xt, basis_y, back_y, wave_yt,
    coef, pot, corn, weig,
    s1, r1, s2, r2, psi, sr, rs1, rs2, ss, ys, sb, g, green, pk, pr, wst, pick, part, o, f,
    load_sem, a1_s, a1_r, a2, pt_s, pt_r, t1_s, t1_r, t2_s, t2_r, sf, bk_s, bk_r, g1_s, g1_r, g2_s, g2_r, fin,
):
    b = lax.axis_index("band")
    p = lax.axis_index("pw")
    x, c = b // 2, b % 2
    chips = BANDS // 2
    partner = b + 1 - 2 * c
    heavy = p // SRC == b
    others = pl.ds(0, TILES - 1)

    loads = [(coef_h, coef), (wave_y_h, wave_y)]
    for j in range(SLAB):
        loads.append((potential.at[:, j, :], pot.at[j]))
    for source, target in (
        (corner, corn), (weight, weig), (wave_x_h, wave_x), (wave_z_h, wave_z), (basis_t_h, basis_t), (basis_h, basis),
        (wave_zt_h, wave_zt), (wave_xt_h, wave_xt), (basis_y_h, basis_y), (back_y_h, back_y), (wave_yt_h, wave_yt),
    ):
        loads.append((source, target))
    loads = [pltpu.make_async_copy(a, z, load_sem.at[n]) for n, (a, z) in enumerate(loads)]
    loads[0].start()
    loads[1].start()

    barrier = pltpu.get_barrier_semaphore()

    def greet_pw(k, _):
        pl.semaphore_signal(barrier, inc=1, device_id={"pw": lax.rem(p + k, TILES)}, device_id_type=MESH)
        return 0

    lax.fori_loop(1, TILES, greet_pw, 0)

    def greet_fit(q, _):
        @pl.when(jnp.logical_not(jnp.logical_and(heavy, q == p)))
        def _():
            pl.semaphore_signal(barrier, inc=1, device_id={"band": p // SRC, "pw": q}, device_id_type=MESH)
        return 0

    lax.fori_loop(0, TILES, greet_fit, 0)

    def greet_band(k, _):
        pl.semaphore_signal(barrier, inc=1, device_id={"band": lax.rem(b + k, BANDS)}, device_id_type=MESH)
        return 0

    lax.fori_loop(1, BANDS, greet_band, 0)
    for load in loads[2:]:
        load.start()

    lane = iota((WG, WG), 1)
    masks = []
    for i in range(2):
        reach = as_column(half[i : i + 1, :].astype(F32))
        masks.append(jnp.where(jnp.abs(lane - WG // 2).astype(F32) <= reach, 1.0, 0.0))
    loads[0].wait()
    loads[1].wait()
    loads = loads[2:]
    rows = [
        jnp.concatenate([coef[0, k, i] * (masks[i] * SCALE_IN) for i in range(2)], axis=1) for k in range(2)
    ]
    section = dot3(pair(wave_y), split(jnp.concatenate(rows, axis=0)))
    flat_s1 = s1.reshape(TILES * 16, WG)
    for i in range(2):
        flat_s1[pl.ds(i, 2 * NG, stride=2), :] = section[:, i * WG : (i + 1) * WG]
    r1[p] = s1[p]

    @pl.when(heavy)
    def _():
        pl.semaphore_wait(barrier, TILES - 1 + BANDS - 1 + TILES - 1)

    @pl.when(jnp.logical_not(heavy))
    def _():
        pl.semaphore_wait(barrier, TILES - 1 + BANDS - 1 + TILES)

    def exchange(source, target, send_sem, recv_sem):
        def send(k, _):
            q = lax.rem(p + k, TILES)
            pltpu.make_async_remote_copy(
                source(q), target(p), send_sem, recv_sem, device_id={"pw": q}, device_id_type=MESH
            ).start()
            return 0

        lax.fori_loop(1, TILES, send, 0)

    plane_rows = [pl.ds(4 * j, 4) for j in range(SLAB)]
    for j in range(SLAB):
        exchange(lambda q: s1.at[q, plane_rows[j]], lambda q: r1.at[q, plane_rows[j]], a1_s, a1_r.at[j])

    loads[SLAB].wait()
    loads[SLAB + 1].wait()

    @pl.when(heavy)
    def _():
        flat = pk.reshape(TILES * 16, CAP)
        for k in range(8):
            flat[pl.ds(k, TILES, stride=16), :] = weig[k, 0]
        flat[pl.ds(8, TILES, stride=16), :] = corn[0].astype(F32)

    mode = lambda k: jnp.where(k <= NG // 2, k, k - NG // 2)
    n_y = mode(iota((NG, CAP), 0))
    n_z = mode((p // PER) * CAP + iota((NG, CAP), 1))
    n_x = mode(b * PER + lax.rem(p, PER))
    square = n_y * n_y + n_z * n_z + n_x * n_x
    green[...] = jnp.where(square > 0, HARTREE_SCALE / jnp.maximum(square, 1).astype(F32), 0.0)

    for load in loads[:SLAB] + loads[SLAB + 2 :]:
        load.wait()

    corner_on = jnp.logical_and(iota((NG, NG), 0) == 0, iota((NG, NG), 1) == 0)
    flat_r1 = r1.reshape(TILES * 16, WG)

    def density_step(j):
        drain(r1.at[others, plane_rows[j]], a1_r.at[j])
        rows = [flat_r1[pl.ds(4 * j + n, TILES, stride=16), :] for n in range(4)]
        turned = dot3(pair(wave_x), split(jnp.concatenate(rows, axis=0)))
        turned = jnp.concatenate([turned[:NG], turned[NG:]], axis=1)
        orbital = dot3(split(turned), pair(wave_z))
        psi[j] = orbital
        real, imag = orbital[:, :NG], orbital[:, NG:]
        density = occupation[0] * (real * real + imag * imag)
        mean = jnp.sum(jnp.sum(density, axis=0, keepdims=True), axis=1, keepdims=True) * (1.0 / (NG * NG))
        modes = dot3(split(density - mean), pair(basis_t))
        modes = dot3(pair(basis), split(modes))
        modes = modes + jnp.where(corner_on, NG * mean, 0.0)
        sr[j] = modes.reshape(chips, 2, PER, NG)
        pltpu.make_async_remote_copy(
            sr.at[j, :, 1 - c], rs1.at[j], t1_s.at[j], t1_r.at[j], device_id={"band": partner}, device_id_type=MESH
        ).start()

    def across(j):
        drain(rs1.at[j], t1_r.at[j])
        for k in range(chips):
            rs1[j, k] = rs1[j, k] + sr[j, k, c]

        def send(k, _):
            to = lax.rem(x + k, chips)
            pltpu.make_async_remote_copy(
                rs1.at[j, to], rs2.at[j, x], t2_s.at[j], t2_r.at[j],
                device_id={"band": 2 * to + c}, device_id_type=MESH,
            ).start()
            return 0

        lax.fori_loop(1, chips, send, 0)
        rs2[j, x] = rs1[j, x]

    flat_ss = ss.reshape(SLAB * TILES, CAP)

    def gather_bands(j):
        drain(rs2.at[j, pl.ds(0, chips - 1)], t2_r.at[j])
        total = (rs2[j, 0] + rs2[j, 1]) + (rs2[j, 2] + rs2[j, 3])
        for h in range(2):
            at = j * TILES + h * PER
            flat_ss[at : at + PER, :] = total[:, h * CAP : (h + 1) * CAP]
        exchange(
            lambda q: ss.at[pl.ds(j * TILES + q, 1)], lambda q: ys.at[pl.ds(j * TILES + q, 1)], sf.at[0], sf.at[1]
        )
        ys[j * TILES + p] = ss[j * TILES + p]

    flat_s2 = s2.reshape(TILES * 16, WG)

    def product_step(j):
        value = pot[j]
        field = psi[j] * jnp.concatenate([value, value], axis=1)
        rows = dot3(split(field), pair(wave_zt))
        rows = jnp.concatenate([rows[:, :WG], rows[:, WG:]], axis=0)
        rows = dot3(pair(wave_xt), split(rows))
        for n in range(4):
            flat_s2[pl.ds(4 * j + n, TILES, stride=16), :] = rows[n * TILES : (n + 1) * TILES]

    def product_send(j):
        exchange(lambda q: s2.at[q, plane_rows[j]], lambda q: r2.at[q, plane_rows[j]], a2.at[0], a2.at[1])

    density_step(0)
    product_step(0)
    density_step(1)
    across(0)
    product_step(1)
    density_step(2)
    across(1)
    gather_bands(0)
    product_step(2)
    density_step(3)

    across(2)
    gather_bands(1)
    across(3)
    gather_bands(2)
    gather_bands(3)
    @pl.when(heavy)
    def _():
        def send(k, _):
            q = lax.rem(p + k, TILES)
            pltpu.make_async_remote_copy(
                pk.at[q, pl.ds(0, 9)], pr.at[p % SRC, pl.ds(0, 9)], pt_s, pt_r.at[p % SRC],
                device_id={"pw": q}, device_id_type=MESH,
            ).start()
            return 0

        lax.fori_loop(1, TILES, send, 0)
        pr[p % SRC, 0:9] = pk[p, 0:9]


    product_step(3)

    r2[p] = s2[p]

    drain(ys.at[pl.ds(0, SLAB * (TILES - 1))], sf.at[1])
    lines = ys.reshape(SLAB * TILES, CAP)[...]
    mean = jnp.sum(lines, axis=0, keepdims=True) * (1.0 / NG)
    modes = dot3(pair(basis_y), split(lines - mean))
    modes = modes + jnp.where(iota((NG, CAP), 0) == 0, math.sqrt(NG) * mean, 0.0)
    sb.reshape((SLAB + 1) * TILES, CAP)[...] = dot3(pair(back_y), split(modes * green[...]))
    for n, group in enumerate(GROUPS):
        exchange(lambda q: sb.at[group, q], lambda q: g.at[group, b, q], bk_s, bk_r.at[n])
        g[group, b, p] = sb[group, p]

    product_send(0)
    product_send(1)
    product_send(2)
    product_send(3)
    def point_step(i):
        @pl.when(SRC * b + i != p)
        def _():
            drain(pr.at[i, pl.ds(0, 9)], pt_r.at[i])

        data = pr[i, 0:9]
        place = data[8:9].astype(jnp.int32)
        at_x = place // (SLAB * NG)
        at_y = lax.rem(place // NG, SLAB)
        at_z = lax.rem(place, NG)
        grid = iota((NG, CAP), 0)
        on = [grid == at_x, grid == lax.rem(at_x + 1, NG)]
        for dz in range(2):
            cell = jnp.where(grid == lax.rem(at_z + dz, NG), 1.0, 0.0)
            pick[i, :, dz * CAP : (dz + 1) * CAP] = cell.astype(BF16)
            for y in range(SLAB + 1):
                value = []
                for dx in range(2):
                    first = jnp.where(at_y == y, data[4 * dx + dz : 4 * dx + dz + 1], 0.0)
                    value.append(jnp.where(at_y == y - 1, data[4 * dx + 2 + dz : 4 * dx + 3 + dz], first))
                value = jnp.where(on[0], value[0], jnp.where(on[1], value[1], 0.0))
                wst[i, y, :, dz * CAP : (dz + 1) * CAP] = value
        part[i] = jnp.zeros((8, 2 * CAP), F32)

    for i in range(SRC):
        point_step(i)

    def modes_of(y, band):
        return g.at[GROUPS[y], band]

    def pass_on(y, k):
        block = modes_of(y, lax.rem(x + chips - k, chips) * 2 + c)
        pltpu.make_async_remote_copy(
            block, block, g2_s.at[y, k], g2_r.at[y, k], device_id={"band": partner}, device_id_type=MESH
        ).start()

    def gather_start(y):
        drain(g.at[GROUPS[y], 0, others], bk_r.at[y])

        def send_x(k, _):
            to = lax.rem(x + k, chips)
            pltpu.make_async_remote_copy(
                modes_of(y, b), modes_of(y, b), g1_s.at[y, k], g1_r.at[y, k],
                device_id={"band": 2 * to + c}, device_id_type=MESH,
            ).start()
            return 0

        lax.fori_loop(1, chips, send_x, 0)
        pass_on(y, 0)

    def forward(y):
        def step(k, _):
            drain(modes_of(y, lax.rem(x + chips - k, chips) * 2 + c), g1_r.at[y, k])
            pass_on(y, k)
            return 0

        lax.fori_loop(1, chips, step, 0)

    flat_g = g.reshape((SLAB + 1) * BANDS * TILES, CAP)

    def group_step(y):
        def arrived(k, _):
            drain(modes_of(y, lax.rem(x + chips - k, chips) * 2 + 1 - c), g2_r.at[y, k])
            return 0

        lax.fori_loop(0, chips, arrived, 0)

    def plane_step(y):
        rows = flat_g[y * BANDS * TILES : (y + 1) * BANDS * TILES, :].reshape(BANDS, 2, PER, CAP)
        modes = jnp.concatenate([rows[:, h].reshape(NG, CAP) for h in range(2)], axis=1)
        plane = dot3(pair(basis_t), split(modes))
        high, low = split(dot3(split(plane), pair(basis)))

        for i in range(SRC):
            lines = dot(high, pick[i]) + dot(low, pick[i])
            lines = (lines * wst[i, y]).reshape(NG // 8, 8, 2 * CAP)
            part[i] = part[i] + jnp.sum(lines, axis=0)

    for n in range(len(GROUPS)):
        gather_start(n)
    for n in range(len(GROUPS)):
        forward(n)
    for n, group in enumerate(GROUPS):
        group_step(n)
        for y in range(group.start, group.start + group.size):
            plane_step(y)

    def fit_sum(i, _):
        lines = jnp.sum(part[i], axis=0, keepdims=True)
        o[i] = lines[:, :CAP] + lines[:, CAP:]
        return 0

    lax.fori_loop(0, SRC, fit_sum, 0)

    def fit_send(n, _):
        to, i = n // SRC, lax.rem(n, SRC)

        @pl.when(jnp.logical_not(jnp.logical_and(to == b, SRC * b + i == p)))
        def _():
            pltpu.make_async_remote_copy(
                o.at[i], f.at[p], fin.at[0], fin.at[1],
                device_id={"band": to, "pw": SRC * b + i}, device_id_type=MESH,
            ).start()
        return 0

    lax.fori_loop(0, BANDS * SRC, fit_send, 0)

    @pl.when(heavy)
    def _():
        f[p] = o[p % SRC]

    drain(r2.at[others], a2.at[1])
    flat_r2 = r2.reshape(TILES * 16, WG)
    cube = jnp.concatenate([flat_r2[pl.ds(i, 2 * NG, stride=2), :] for i in range(2)], axis=1)
    cube = dot3(pair(wave_yt), split(cube))
    for k in range(2):
        for i in range(2):
            action[0, k, i] = cube[k * WG : (k + 1) * WG, i * WG : (i + 1) * WG] * (masks[i] * SCALE_OUT)

    drain(s1.at[others], a1_s)
    drain(s2.at[others], a2.at[0])
    drain(ss.at[pl.ds(0, SLAB * (TILES - 1))], sf.at[0])
    drain(sb.at[:, others], bk_s)

    @pl.when(heavy)
    def _():
        drain(pk.at[others, pl.ds(0, 9)], pt_s)

    def sent(j, _):
        drain(rs1.at[j], t1_s.at[j])
        drain(rs1.at[j, pl.ds(0, chips - 1)], t2_s.at[j])
        return 0

    lax.fori_loop(0, SLAB, sent, 0)

    def passed(y):
        for k in range(chips):
            drain(modes_of(y, b), g2_s.at[y, k])
            if k > 0:
                drain(modes_of(y, b), g1_s.at[y, k])

    for y in range(len(GROUPS)):
        passed(y)

    @pl.when(heavy)
    def _():
        drain(f.at[others], fin.at[1])
        drain(f.at[others], fin.at[0])

    @pl.when(jnp.logical_not(heavy))
    def _():
        drain(f, fin.at[1])
        drain(f, fin.at[0])

    live = iota((TILES, CAP), 1).astype(F32) < as_column(count[...].astype(F32))
    fit[0] = jnp.where(live, f.reshape(TILES, CAP)[...], 0.0)


def body(coefficients, halfwidth, occupation, potential, corner, weight, count):
    held = {name: jnp.asarray(table) for name, table in tables().items()}
    late = [held[name] for name in LATE]
    vmem = pl.BlockSpec(memory_space=pltpu.VMEM)
    anywhere = pl.BlockSpec(memory_space=pl.ANY)
    dma = pltpu.SemaphoreType.DMA
    block = lambda *shape: pltpu.VMEM(shape, F32)
    short = lambda *shape: pltpu.VMEM(shape, BF16)
    scratch = [short(*table.shape) for table in late]
    scratch += [
        block(*coefficients.shape),
        block(SLAB, NG, NG),
        pltpu.VMEM((1, TILES, CAP), jnp.int32),
        block(8, 1, TILES, CAP),
        block(TILES, 16, WG),
        block(TILES, 16, WG),
        block(TILES, 16, WG),
        block(TILES, 16, WG),
        block(SLAB, NG, 2 * NG),
        block(SLAB, BANDS // 2, 2, PER, NG),
        block(SLAB, BANDS // 2, PER, NG),
        block(SLAB, BANDS // 2, PER, NG),
        block(SLAB * TILES, 1, CAP),
        block(SLAB * TILES, 1, CAP),
        block(SLAB + 1, TILES, 1, CAP),
        block(SLAB + 1, BANDS, TILES, 1, CAP),
        block(NG, CAP),
        block(TILES, 16, CAP),
        block(SRC, 16, CAP),
        block(SRC, SLAB + 1, NG, 2 * CAP),
        short(SRC, NG, 2 * CAP),
        block(SRC, 8, 2 * CAP),
        block(SRC, 1, CAP),
        block(TILES, 1, CAP),
    ]
    planes = (len(GROUPS), BANDS // 2)
    scratch += [
        dma((SLAB + 3 + len(late),)),
        dma(()), dma((SLAB,)), dma((2,)),
        dma(()), dma((SRC,)),
        dma((SLAB,)), dma((SLAB,)), dma((SLAB,)), dma((SLAB,)),
        dma((2,)), dma(()), dma((len(GROUPS),)),
        dma(planes), dma(planes), dma(planes), dma(planes),
        dma((2,)),
    ]
    return pl.pallas_call(
        kernel,
        out_shape=(
            jax.ShapeDtypeStruct(coefficients.shape, F32),
            jax.ShapeDtypeStruct(corner.shape, F32),
        ),
        in_specs=[vmem, pl.BlockSpec(memory_space=pltpu.SMEM), vmem, anywhere] + [anywhere] * (3 + len(late)),
        out_specs=(vmem, vmem),
        scratch_shapes=scratch,
        compiler_params=pltpu.CompilerParams(
            collective_id=0, has_side_effects=True, vmem_limit_bytes=60 * 1024 * 1024
        ),
    )(halfwidth, occupation, count, coefficients, *late[:1], potential, corner, weight, *late[1:])


def solution(mesh):
    placed = (
        P("band", None, "pw", None, None),
        P("pw", None),
        P("band"),
        P(None, "pw", None),
        P("pw", None, None),
        P(None, "pw", None, None),
        P("pw", None),
    )
    return jax.shard_map(
        body,
        mesh=mesh,
        in_specs=placed,
        out_specs=(P("band", None, "pw", None, None), P("pw", None, None)),
        check_vma=False,
    )
```

```python
import math

import jax
import jax.numpy as jnp
import ml_dtypes
import numpy as np
from jax import lax
from jax.experimental import pallas as pl
from jax.experimental.pallas import tpu as pltpu
from jax.sharding import PartitionSpec as P

HARTREE_SCALE = 200.0
MESH = pl.DeviceIdType.MESH
F32 = jnp.float32
BF16 = jnp.bfloat16

NG = 256
WG = 128
BANDS = 8
TILES = 64
SLAB = 4
CAP = 128
PER = NG // BANDS
SRC = TILES // BANDS
GROUPS = (pl.ds(0, 3), pl.ds(3, 2))
SCALE_IN = float(WG) ** -1.5
SCALE_OUT = float(WG) ** 1.5 / float(NG) ** 3


def halves_of(table):
    high = np.asarray(table, np.float64).astype(ml_dtypes.bfloat16)
    low = (table - high.astype(np.float64)).astype(ml_dtypes.bfloat16)
    return np.stack([high, low])


def tables():
    position = np.arange(NG)
    modes = np.arange(WG) - WG // 2
    angle = (np.outer(position, modes) % NG) * (2.0 * math.pi / NG)
    cosine, sine = np.cos(angle), np.sin(angle)
    wave = np.stack([np.stack([cosine, -sine], 1), np.stack([sine, cosine], 1)], 0)
    wave_y = wave.reshape(2, TILES, SLAB, 2, WG).transpose(1, 2, 0, 3, 4).reshape(2 * NG, 2 * WG)
    wave_x = wave.reshape(2, NG, 2, TILES, 2).transpose(0, 1, 2, 4, 3).reshape(2 * NG, 2 * WG)
    wave_z = wave.transpose(2, 3, 0, 1).reshape(2 * WG, 2 * NG)
    angle = lambda n: (np.outer(n, position) % NG) * (2.0 * math.pi / NG)
    rows = np.concatenate([np.cos(angle(np.arange(NG // 2 + 1))), np.sin(angle(np.arange(1, NG // 2)))])
    basis = rows / np.sqrt(np.sum(rows * rows, axis=1, keepdims=True))
    basis_y = basis.reshape(NG, TILES, SLAB).transpose(0, 2, 1).reshape(NG, NG)
    planes = (np.arange(TILES)[None, :] * SLAB + np.arange(SLAB + 1)[:, None]) % NG
    named = dict(
        wave_y=wave_y,
        wave_x=wave_x,
        wave_z=wave_z,
        basis_t=basis.T,
        basis=basis,
        basis_y=basis_y,
        back_y=basis.T[planes.reshape(-1)],
        wave_zt=wave_z.T,
        wave_xt=wave_x.T,
        wave_yt=wave_y.T,
    )
    return {name: halves_of(table) for name, table in named.items()}


LATE = ("wave_y", "wave_x", "wave_z", "basis_t", "basis", "wave_zt", "wave_xt", "basis_y", "back_y", "wave_yt")


def split(value):
    high = value.astype(BF16)
    return high, (value - high.astype(F32)).astype(BF16)


def dot(left, right):
    return jnp.dot(left, right, preferred_element_type=F32)


def dot3(left, right):
    return dot(left[0], right[0]) + (dot(left[0], right[1]) + dot(left[1], right[0]))


def pair(ref):
    return ref[0], ref[1]


def iota(shape, dim):
    return lax.broadcasted_iota(jnp.int32, shape, dim)


def as_column(row):
    size = row.shape[1]
    on = iota((size, size), 0) == iota((size, size), 1)
    return jnp.sum(jnp.where(on, jnp.broadcast_to(row, (size, size)), 0.0), axis=1, keepdims=True)


def drain(ref, sem):
    pltpu.make_async_copy(ref, ref, sem).wait()


def kernel(
    half, occupation, count,
    coef_h, wave_y_h, potential, corner, weight, wave_x_h, wave_z_h, basis_t_h, basis_h, wave_zt_h, wave_xt_h,
    basis_y_h, back_y_h, wave_yt_h,
    action, fit,
    wave_y, wave_x, wave_z, basis_t, basis, wave_zt, wave_xt, basis_y, back_y, wave_yt,
    coef, pot, corn, weig,
    s1, r1, s2, r2, psi, sr, rs1, rs2, ss, ys, sb, g, green, pk, pr, wst, pick, part, o, f, f2,
    load_sem, a1_s, a1_r, a2, pt_s, pt_r, t1_s, t1_r, t2_s, t2_r, sf, bk_s, bk_r, g1_s, g1_r, g2_s, g2_r, fin, fan,
):
    b = lax.axis_index("band")
    p = lax.axis_index("pw")
    x, c = b // 2, b % 2
    chips = BANDS // 2
    partner = b + 1 - 2 * c
    heavy = p // SRC == b
    others = pl.ds(0, TILES - 1)

    loads = [(coef_h, coef), (wave_y_h, wave_y)]
    for j in range(SLAB):
        loads.append((potential.at[:, j, :], pot.at[j]))
    for source, target in (
        (corner, corn), (weight, weig), (wave_x_h, wave_x), (wave_z_h, wave_z), (basis_t_h, basis_t), (basis_h, basis),
        (wave_zt_h, wave_zt), (wave_xt_h, wave_xt), (basis_y_h, basis_y), (back_y_h, back_y), (wave_yt_h, wave_yt),
    ):
        loads.append((source, target))
    loads = [pltpu.make_async_copy(a, z, load_sem.at[n]) for n, (a, z) in enumerate(loads)]
    loads[0].start()
    loads[1].start()

    barrier = pltpu.get_barrier_semaphore()

    def greet_pw(k, _):
        pl.semaphore_signal(barrier, inc=1, device_id={"pw": lax.rem(p + k, TILES)}, device_id_type=MESH)
        return 0

    lax.fori_loop(1, TILES, greet_pw, 0)

    def greet_band(k, _):
        pl.semaphore_signal(barrier, inc=1, device_id={"band": lax.rem(b + k, BANDS)}, device_id_type=MESH)
        return 0

    lax.fori_loop(1, BANDS, greet_band, 0)
    for load in loads[2:]:
        load.start()

    lane = iota((WG, WG), 1)
    masks = []
    for i in range(2):
        reach = as_column(half[i : i + 1, :].astype(F32))
        masks.append(jnp.where(jnp.abs(lane - WG // 2).astype(F32) <= reach, 1.0, 0.0))
    loads[0].wait()
    loads[1].wait()
    loads = loads[2:]
    rows = [
        jnp.concatenate([coef[0, k, i] * (masks[i] * SCALE_IN) for i in range(2)], axis=1) for k in range(2)
    ]
    section = dot3(pair(wave_y), split(jnp.concatenate(rows, axis=0)))
    flat_s1 = s1.reshape(TILES * 16, WG)
    for i in range(2):
        flat_s1[pl.ds(i, 2 * NG, stride=2), :] = section[:, i * WG : (i + 1) * WG]
    r1[p] = s1[p]

    pl.semaphore_wait(barrier, TILES - 1 + BANDS - 1)

    def exchange(source, target, send_sem, recv_sem):
        def send(k, _):
            q = lax.rem(p + k, TILES)
            pltpu.make_async_remote_copy(
                source(q), target(p), send_sem, recv_sem, device_id={"pw": q}, device_id_type=MESH
            ).start()
            return 0

        lax.fori_loop(1, TILES, send, 0)

    plane_rows = [pl.ds(4 * j, 4) for j in range(SLAB)]
    for j in range(SLAB):
        exchange(lambda q: s1.at[q, plane_rows[j]], lambda q: r1.at[q, plane_rows[j]], a1_s, a1_r.at[j])

    loads[SLAB].wait()
    loads[SLAB + 1].wait()

    @pl.when(heavy)
    def _():
        flat = pk.reshape(TILES * 16, CAP)
        for k in range(8):
            flat[pl.ds(k, TILES, stride=16), :] = weig[k, 0]
        flat[pl.ds(8, TILES, stride=16), :] = corn[0].astype(F32)

    mode = lambda k: jnp.where(k <= NG // 2, k, k - NG // 2)
    n_y = mode(iota((NG, CAP), 0))
    n_z = mode((p // PER) * CAP + iota((NG, CAP), 1))
    n_x = mode(b * PER + lax.rem(p, PER))
    square = n_y * n_y + n_z * n_z + n_x * n_x
    green[...] = jnp.where(square > 0, HARTREE_SCALE / jnp.maximum(square, 1).astype(F32), 0.0)

    for load in loads[:SLAB] + loads[SLAB + 2 :]:
        load.wait()

    corner_on = jnp.logical_and(iota((NG, NG), 0) == 0, iota((NG, NG), 1) == 0)
    flat_r1 = r1.reshape(TILES * 16, WG)

    def density_step(j):
        drain(r1.at[others, plane_rows[j]], a1_r.at[j])
        rows = [flat_r1[pl.ds(4 * j + n, TILES, stride=16), :] for n in range(4)]
        turned = dot3(pair(wave_x), split(jnp.concatenate(rows, axis=0)))
        turned = jnp.concatenate([turned[:NG], turned[NG:]], axis=1)
        orbital = dot3(split(turned), pair(wave_z))
        psi[j] = orbital
        real, imag = orbital[:, :NG], orbital[:, NG:]
        density = occupation[0] * (real * real + imag * imag)
        mean = jnp.sum(jnp.sum(density, axis=0, keepdims=True), axis=1, keepdims=True) * (1.0 / (NG * NG))
        modes = dot3(split(density - mean), pair(basis_t))
        modes = dot3(pair(basis), split(modes))
        modes = modes + jnp.where(corner_on, NG * mean, 0.0)
        sr[j] = modes.reshape(chips, 2, PER, NG)
        pltpu.make_async_remote_copy(
            sr.at[j, :, 1 - c], rs1.at[j], t1_s.at[j], t1_r.at[j], device_id={"band": partner}, device_id_type=MESH
        ).start()

    def across(j):
        drain(rs1.at[j], t1_r.at[j])
        for k in range(chips):
            rs1[j, k] = rs1[j, k] + sr[j, k, c]

        def send(k, _):
            to = lax.rem(x + k, chips)
            pltpu.make_async_remote_copy(
                rs1.at[j, to], rs2.at[j, x], t2_s.at[j], t2_r.at[j],
                device_id={"band": 2 * to + c}, device_id_type=MESH,
            ).start()
            return 0

        lax.fori_loop(1, chips, send, 0)
        rs2[j, x] = rs1[j, x]

    flat_ss = ss.reshape(SLAB * TILES, CAP)

    def gather_bands(j):
        drain(rs2.at[j, pl.ds(0, chips - 1)], t2_r.at[j])
        total = (rs2[j, 0] + rs2[j, 1]) + (rs2[j, 2] + rs2[j, 3])
        for h in range(2):
            at = j * TILES + h * PER
            flat_ss[at : at + PER, :] = total[:, h * CAP : (h + 1) * CAP]
        exchange(
            lambda q: ss.at[pl.ds(j * TILES + q, 1)], lambda q: ys.at[pl.ds(j * TILES + q, 1)], sf.at[0], sf.at[1]
        )
        ys[j * TILES + p] = ss[j * TILES + p]

    flat_s2 = s2.reshape(TILES * 16, WG)

    def product_step(j):
        value = pot[j]
        field = psi[j] * jnp.concatenate([value, value], axis=1)
        rows = dot3(split(field), pair(wave_zt))
        rows = jnp.concatenate([rows[:, :WG], rows[:, WG:]], axis=0)
        rows = dot3(pair(wave_xt), split(rows))
        for n in range(4):
            flat_s2[pl.ds(4 * j + n, TILES, stride=16), :] = rows[n * TILES : (n + 1) * TILES]

    def product_send(j):
        exchange(lambda q: s2.at[q, plane_rows[j]], lambda q: r2.at[q, plane_rows[j]], a2.at[0], a2.at[1])

    density_step(0)
    product_step(0)
    density_step(1)
    across(0)
    product_step(1)
    density_step(2)
    across(1)
    gather_bands(0)
    product_step(2)
    density_step(3)

    across(2)
    gather_bands(1)
    across(3)
    gather_bands(2)
    gather_bands(3)
    @pl.when(heavy)
    def _():
        def send(k, _):
            q = lax.rem(p + k, TILES)
            pltpu.make_async_remote_copy(
                pk.at[q, pl.ds(0, 9)], pr.at[p % SRC, pl.ds(0, 9)], pt_s, pt_r.at[p % SRC],
                device_id={"pw": q}, device_id_type=MESH,
            ).start()
            return 0

        lax.fori_loop(1, TILES, send, 0)
        pr[p % SRC, 0:9] = pk[p, 0:9]


    product_step(3)

    r2[p] = s2[p]

    drain(ys.at[pl.ds(0, SLAB * (TILES - 1))], sf.at[1])
    lines = ys.reshape(SLAB * TILES, CAP)[...]
    mean = jnp.sum(lines, axis=0, keepdims=True) * (1.0 / NG)
    modes = dot3(pair(basis_y), split(lines - mean))
    modes = modes + jnp.where(iota((NG, CAP), 0) == 0, math.sqrt(NG) * mean, 0.0)
    sb.reshape((SLAB + 1) * TILES, CAP)[...] = dot3(pair(back_y), split(modes * green[...]))
    for n, group in enumerate(GROUPS):
        exchange(lambda q: sb.at[group, q], lambda q: g.at[group, b, q], bk_s, bk_r.at[n])
        g[group, b, p] = sb[group, p]

    product_send(0)
    product_send(1)
    product_send(2)
    product_send(3)
    def point_step(i):
        @pl.when(SRC * b + i != p)
        def _():
            drain(pr.at[i, pl.ds(0, 9)], pt_r.at[i])

        data = pr[i, 0:9]
        place = data[8:9].astype(jnp.int32)
        at_x = place // (SLAB * NG)
        at_y = lax.rem(place // NG, SLAB)
        at_z = lax.rem(place, NG)
        grid = iota((NG, CAP), 0)
        on = [grid == at_x, grid == lax.rem(at_x + 1, NG)]
        for dz in range(2):
            cell = jnp.where(grid == lax.rem(at_z + dz, NG), 1.0, 0.0)
            pick[i, :, dz * CAP : (dz + 1) * CAP] = cell.astype(BF16)
            for y in range(SLAB + 1):
                value = []
                for dx in range(2):
                    first = jnp.where(at_y == y, data[4 * dx + dz : 4 * dx + dz + 1], 0.0)
                    value.append(jnp.where(at_y == y - 1, data[4 * dx + 2 + dz : 4 * dx + 3 + dz], first))
                value = jnp.where(on[0], value[0], jnp.where(on[1], value[1], 0.0))
                wst[i, y, :, dz * CAP : (dz + 1) * CAP] = value
        part[i] = jnp.zeros((8, 2 * CAP), F32)

    for i in range(SRC):
        point_step(i)

    def modes_of(y, band):
        return g.at[GROUPS[y], band]

    def pass_on(y, k):
        block = modes_of(y, lax.rem(x + chips - k, chips) * 2 + c)
        pltpu.make_async_remote_copy(
            block, block, g2_s.at[y, k], g2_r.at[y, k], device_id={"band": partner}, device_id_type=MESH
        ).start()

    def gather_start(y):
        drain(g.at[GROUPS[y], 0, others], bk_r.at[y])

        def send_x(k, _):
            to = lax.rem(x + k, chips)
            pltpu.make_async_remote_copy(
                modes_of(y, b), modes_of(y, b), g1_s.at[y, k], g1_r.at[y, k],
                device_id={"band": 2 * to + c}, device_id_type=MESH,
            ).start()
            return 0

        lax.fori_loop(1, chips, send_x, 0)
        pass_on(y, 0)

    def forward(y):
        def step(k, _):
            drain(modes_of(y, lax.rem(x + chips - k, chips) * 2 + c), g1_r.at[y, k])
            pass_on(y, k)
            return 0

        lax.fori_loop(1, chips, step, 0)

    flat_g = g.reshape((SLAB + 1) * BANDS * TILES, CAP)

    def group_step(y):
        def arrived(k, _):
            drain(modes_of(y, lax.rem(x + chips - k, chips) * 2 + 1 - c), g2_r.at[y, k])
            return 0

        lax.fori_loop(0, chips, arrived, 0)

    def plane_step(y):
        rows = flat_g[y * BANDS * TILES : (y + 1) * BANDS * TILES, :].reshape(BANDS, 2, PER, CAP)
        modes = jnp.concatenate([rows[:, h].reshape(NG, CAP) for h in range(2)], axis=1)
        plane = dot3(pair(basis_t), split(modes))
        high, low = split(dot3(split(plane), pair(basis)))

        for i in range(SRC):
            lines = dot(high, pick[i]) + dot(low, pick[i])
            lines = (lines * wst[i, y]).reshape(NG // 8, 8, 2 * CAP)
            part[i] = part[i] + jnp.sum(lines, axis=0)

    for n in range(len(GROUPS)):
        gather_start(n)
    for n in range(len(GROUPS)):
        forward(n)
    for n, group in enumerate(GROUPS):
        group_step(n)
        for y in range(group.start, group.start + group.size):
            plane_step(y)

    def fit_sum(i, _):
        lines = jnp.sum(part[i], axis=0, keepdims=True)
        o[i] = lines[:, :CAP] + lines[:, CAP:]
        return 0

    lax.fori_loop(0, SRC, fit_sum, 0)

    def fit_send(i, _):
        @pl.when(SRC * b + i != p)
        def _():
            pltpu.make_async_remote_copy(
                o.at[i], f.at[p], fin.at[0], fin.at[1], device_id={"pw": SRC * b + i}, device_id_type=MESH
            ).start()
        return 0

    lax.fori_loop(0, SRC, fit_send, 0)

    drain(r2.at[others], a2.at[1])
    flat_r2 = r2.reshape(TILES * 16, WG)
    cube = jnp.concatenate([flat_r2[pl.ds(i, 2 * NG, stride=2), :] for i in range(2)], axis=1)
    cube = dot3(pair(wave_yt), split(cube))
    for k in range(2):
        for i in range(2):
            action[0, k, i] = cube[k * WG : (k + 1) * WG, i * WG : (i + 1) * WG] * (masks[i] * SCALE_OUT)

    @pl.when(heavy)
    def _():
        f[p] = o[p % SRC]
        drain(f.at[others], fin.at[1])

        def spread(k, _):
            pltpu.make_async_remote_copy(
                f, f2, fan.at[0], fan.at[1], device_id={"band": lax.rem(b + k, BANDS)}, device_id_type=MESH
            ).start()
            return 0

        lax.fori_loop(1, BANDS, spread, 0)
        f2[...] = f[...]

    drain(s1.at[others], a1_s)
    drain(s2.at[others], a2.at[0])
    drain(ss.at[pl.ds(0, SLAB * (TILES - 1))], sf.at[0])
    drain(sb.at[:, others], bk_s)

    @pl.when(heavy)
    def _():
        drain(pk.at[others, pl.ds(0, 9)], pt_s)

    def sent(j, _):
        drain(rs1.at[j], t1_s.at[j])
        drain(rs1.at[j, pl.ds(0, chips - 1)], t2_s.at[j])
        return 0

    lax.fori_loop(0, SLAB, sent, 0)

    def passed(y):
        for k in range(chips):
            drain(modes_of(y, b), g2_s.at[y, k])
            if k > 0:
                drain(modes_of(y, b), g1_s.at[y, k])

    for y in range(len(GROUPS)):
        passed(y)

    @pl.when(heavy)
    def _():
        drain(o.at[pl.ds(0, SRC - 1)], fin.at[0])
        drain(g.at[0, pl.ds(0, BANDS - 1)], fan.at[0])

    @pl.when(jnp.logical_not(heavy))
    def _():
        drain(o, fin.at[0])
        drain(f2, fan.at[1])

    live = iota((TILES, CAP), 1).astype(F32) < as_column(count[...].astype(F32))
    fit[0] = jnp.where(live, f2.reshape(TILES, CAP)[...], 0.0)


def body(coefficients, halfwidth, occupation, potential, corner, weight, count):
    held = {name: jnp.asarray(table) for name, table in tables().items()}
    late = [held[name] for name in LATE]
    vmem = pl.BlockSpec(memory_space=pltpu.VMEM)
    anywhere = pl.BlockSpec(memory_space=pl.ANY)
    dma = pltpu.SemaphoreType.DMA
    block = lambda *shape: pltpu.VMEM(shape, F32)
    short = lambda *shape: pltpu.VMEM(shape, BF16)
    scratch = [short(*table.shape) for table in late]
    scratch += [
        block(*coefficients.shape),
        block(SLAB, NG, NG),
        pltpu.VMEM((1, TILES, CAP), jnp.int32),
        block(8, 1, TILES, CAP),
        block(TILES, 16, WG),
        block(TILES, 16, WG),
        block(TILES, 16, WG),
        block(TILES, 16, WG),
        block(SLAB, NG, 2 * NG),
        block(SLAB, BANDS // 2, 2, PER, NG),
        block(SLAB, BANDS // 2, PER, NG),
        block(SLAB, BANDS // 2, PER, NG),
        block(SLAB * TILES, 1, CAP),
        block(SLAB * TILES, 1, CAP),
        block(SLAB + 1, TILES, 1, CAP),
        block(SLAB + 1, BANDS, TILES, 1, CAP),
        block(NG, CAP),
        block(TILES, 16, CAP),
        block(SRC, 16, CAP),
        block(SRC, SLAB + 1, NG, 2 * CAP),
        short(SRC, NG, 2 * CAP),
        block(SRC, 8, 2 * CAP),
        block(SRC, 1, CAP),
        block(TILES, 1, CAP),
        block(TILES, 1, CAP),
    ]
    planes = (len(GROUPS), BANDS // 2)
    scratch += [
        dma((SLAB + 3 + len(late),)),
        dma(()), dma((SLAB,)), dma((2,)),
        dma(()), dma((SRC,)),
        dma((SLAB,)), dma((SLAB,)), dma((SLAB,)), dma((SLAB,)),
        dma((2,)), dma(()), dma((len(GROUPS),)),
        dma(planes), dma(planes), dma(planes), dma(planes),
        dma((2,)), dma((2,)),
    ]
    return pl.pallas_call(
        kernel,
        out_shape=(
            jax.ShapeDtypeStruct(coefficients.shape, F32),
            jax.ShapeDtypeStruct(corner.shape, F32),
        ),
        in_specs=[vmem, pl.BlockSpec(memory_space=pltpu.SMEM), vmem, anywhere] + [anywhere] * (3 + len(late)),
        out_specs=(vmem, vmem),
        scratch_shapes=scratch,
        compiler_params=pltpu.CompilerParams(
            collective_id=0, has_side_effects=True, vmem_limit_bytes=60 * 1024 * 1024
        ),
    )(halfwidth, occupation, count, coefficients, *late[:1], potential, corner, weight, *late[1:])


def solution(mesh):
    placed = (
        P("band", None, "pw", None, None),
        P("pw", None),
        P("band"),
        P(None, "pw", None),
        P("pw", None, None),
        P(None, "pw", None, None),
        P("pw", None),
    )
    return jax.shard_map(
        body,
        mesh=mesh,
        in_specs=placed,
        out_specs=(P("band", None, "pw", None, None), P("pw", None, None)),
        check_vma=False,
    )
```
